32 devices in a mesh: dp: 4 (over z), space: 8 (over y, x, core).
Axes of the slice: x: 2, y: 2, z: 4, core: 2. Of those that a mesh axis runs over, the one named last changes fastest.
Arguments:
- volume: bfloat16 [4, 8, 8, 64, 16, 256], P('dp', 'space'), may hold values from -6 to 6
- fine_filter: bfloat16 [3, 3, 3, 256, 256], P(None, None, None, 'dp'), may hold values from -0.078125 to 0.078125
- coarse_filter: bfloat16 [3, 3, 3, 256, 256], P(None, None, None, 'dp'), may hold values from -0.078125 to 0.078125
- fine_bias: float32 [256], replicated, may hold values from -3 to 3
- coarse_bias: float32 [256], replicated, may hold values from -3 to 3
Outputs:
- context: bfloat16 [4, 8, 8, 64, 16, 256], P('dp', 'space')
The draws below stay inside these ranges and needn't reach their ends.
All inputs are finite; a program needn't handle non-finite values.
Results may differ from the reference program's by a relative error of at most 0.0047.
Values may be sent and summed in bfloat16 or wider, within the bound.
A program may use at most 192 MiB of HBM per device.

```python
import jax
import jax.numpy as jnp
from jax import lax

C = 256
X = 64
Y = 64
Z = 16
BX = 8
CROPS = 4
GX = 8
GY = 1
BY = 64
BRICKS = 8


def level_of(stream_key, shape, split, least, largest):
    factor_of, own = 1.0, jax.random.fold_in(stream_key, 6)
    for position, blocks in split:
        heights = jnp.exp(jax.random.uniform(jax.random.fold_in(own, position), (blocks,), jnp.float32, least / len(split), largest / len(split)))
        factor_of = factor_of * jnp.repeat(heights, shape[position] // blocks).reshape([-1 if axis == position else 1 for axis in range(len(shape))])
    return factor_of


def noise(rng, shape, scale, most, shards=(), held_as=jnp.bfloat16):
    factor_of = level_of(rng, shape, shards, -0.22, 0.18) if shards else 1.0
    array = jax.random.normal(rng, shape, jnp.float32) * scale * factor_of
    return jnp.minimum(jnp.maximum(array, -most), most).astype(held_as)


def setup_inputs(seed: int = 0) -> dict:
    streams_of = jax.random.split(jax.random.key(seed), 6)
    return {
        "volume": noise(streams_of[0], (CROPS, BRICKS, BX, BY, Z, C), 1.0, 6.0, ((0, 4), (1, 8))),
        "fine_filter": noise(streams_of[1], (3, 3, 3, C, C), (27 * C) ** -0.5, 0.078125, ((3, 4),)),
        "coarse_filter": noise(streams_of[2], (3, 3, 3, C, C), (27 * C) ** -0.5, 0.078125, ((3, 4),)),
        "fine_bias": noise(streams_of[3], (C,), 0.5, 3.0, (), jnp.float32),
        "coarse_bias": noise(streams_of[4], (C,), 0.5, 3.0, (), jnp.float32),
    }


def dilated(crop, filt, bias, rate):
    out = lax.conv_general_dilated(crop[None].astype(jnp.float32), filt.astype(jnp.float32), (1, 1, 1), [(rate, rate)] * 3, rhs_dilation=(rate, rate, rate), dimension_numbers=("NDHWC", "DHWIO", "NDHWC"), precision=lax.Precision.HIGHEST)[0]
    return (crop.astype(jnp.float32) + jax.nn.gelu(out + bias)).astype(jnp.bfloat16)


def reference(volume, fine_filter, coarse_filter, fine_bias, coarse_bias):
    crops = volume.reshape(CROPS, GX, GY, BX, BY, Z, C).transpose(0, 1, 3, 2, 4, 5, 6).reshape(CROPS, X, Y, Z, C)

    def one_crop(crop):
        middle = dilated(crop, fine_filter, fine_bias, 4)
        return dilated(middle, coarse_filter, coarse_bias, 8)

    result = lax.map(one_crop, crops)
    return result.reshape(CROPS, GX, BX, GY, BY, Z, C).transpose(0, 1, 3, 2, 4, 5, 6).reshape(CROPS, GX * GY, BX, BY, Z, C)
```

```python
import jax
import jax.numpy as jnp
from jax import lax
from jax.experimental import pallas as pl
from jax.experimental.pallas import tpu as pltpu
from jax.sharding import PartitionSpec as P

X = 64
BX = 8


def filters(shard):
    return lax.all_gather(shard, "dp", axis=3, tiled=True)


def dense_taps(grid, weights, bias):
    items, length_x, length_y, length_z, channels = grid.shape
    padded = jnp.pad(grid, ((0, 0), (1, 1), (1, 1), (1, 1), (0, 0)))
    total = jnp.zeros(grid.shape, jnp.float32)
    for step_x in range(3):
        for step_y in range(3):
            window = padded[:, step_x : step_x + length_x, step_y : step_y + length_y]
            stacked = jnp.concatenate(
                [window[:, :, :, depth : depth + length_z] for depth in range(3)], axis=-1
            )
            total = total + jnp.dot(
                stacked,
                weights[step_x, step_y].reshape(3 * channels, channels),
                preferred_element_type=jnp.float32,
            )
    return (grid.astype(jnp.float32) + jax.nn.gelu(total + bias)).astype(jnp.bfloat16)


def fine_cosets(brick):
    size_x, size_y, size_z, channels = brick.shape
    split = brick.reshape(size_x // 4, 4, size_y // 4, 4, size_z // 4, 4, channels)
    return split.transpose(1, 3, 5, 0, 2, 4, 6).reshape(
        64, size_x // 4, size_y // 4, size_z // 4, channels
    )


def fine_bricks(cosets):
    count, along_u, along_v, along_w, channels = cosets.shape
    split = cosets.reshape(4, 4, 4, along_u, along_v, along_w, channels).transpose(
        3, 0, 4, 1, 5, 2, 6
    )
    return split.reshape(along_u * 4, along_v * 4, along_w * 4, channels)


def assemble(parts):
    items, devices, along_u, along_v, along_w, channels = parts.shape
    across_x = X // BX
    across_y = devices // across_x
    grid = parts.reshape(items, across_x, across_y, along_u, along_v, along_w, channels).transpose(
        0, 1, 3, 2, 4, 5, 6
    )
    return grid.reshape(items, across_x * along_u, across_y * along_v, along_w, channels)


def disassemble(grid, along_u, along_v):
    items, size_x, size_y, along_w, channels = grid.shape
    across_x = size_x // along_u
    across_y = size_y // along_v
    parts = grid.reshape(items, across_x, along_u, across_y, along_v, along_w, channels).transpose(
        0, 1, 3, 2, 4, 5, 6
    )
    return parts.reshape(1, items, across_x * across_y, along_u, along_v, along_w, channels)


def split_halves(grid):
    items, size_x, size_y, size_z, channels = grid.shape
    parts = grid.reshape(items, size_x // 2, 2, size_y // 2, 2, size_z // 2, 2, channels).transpose(
        0, 2, 4, 6, 1, 3, 5, 7
    )
    return parts.reshape(items * 8, size_x // 2, size_y // 2, size_z // 2, channels)


def join_halves(parts, items):
    count, half_x, half_y, half_z, channels = parts.shape
    grid = parts.reshape(items, 2, 2, 2, half_x, half_y, half_z, channels).transpose(
        0, 4, 1, 5, 2, 6, 3, 7
    )
    return grid.reshape(items, half_x * 2, half_y * 2, half_z * 2, channels)


MESH = pl.DeviceIdType.MESH
N = 8
S = 16
F32 = jnp.float32


def place(owner, k):
    number = 2 * owner + k
    return lax.div(number, 4), lax.rem(number, 4)


def spread(rows, shift):
    zero = jnp.zeros((S, shift, rows.shape[-1]), F32)
    before = jnp.concatenate([zero, rows[:, : S - shift]], axis=1)
    after = jnp.concatenate([rows[:, shift:], zero], axis=1)
    return before.astype(jnp.bfloat16), after.astype(jnp.bfloat16)


def taps(grid, x, step, weights):
    acc = None
    for dx in range(3):
        for dy in range(3):
            lhs = grid[x + dx * step, pl.ds(dy * step, S)].reshape(S * S, 768)
            part = jnp.dot(lhs, weights[3 * dx + dy], preferred_element_type=F32)
            acc = part if acc is None else acc + part
    return acc


def fill(grid, x, pad, rows, shift):
    before, after = spread(rows.astype(F32), shift)
    grid[x, pl.ds(pad, S), :, 0:256] = before
    grid[x, pl.ds(pad, S), :, 256:512] = rows
    grid[x, pl.ds(pad, S), :, 512:768] = after


def clear(grid, pad):
    side = S + 2 * pad
    for edge in list(range(pad)) + list(range(S + pad, side)):
        grid[edge] = jnp.zeros((side, S, 768), jnp.bfloat16)

    @pl.loop(pad, S + pad)
    def _(x):
        grid[x, 0:pad] = jnp.zeros((pad, S, 768), jnp.bfloat16)
        grid[x, S + pad : side] = jnp.zeros((pad, S, 768), jnp.bfloat16)


def kernel(
    vol, fw, cw, fb, cb, out, recv, fine, coarse, done,
    in_send, in_recv, in_own, out_send, out_recv, out_own,
):
    me = lax.axis_index("space")

    barrier = pltpu.get_barrier_semaphore()
    for s in range(1, N):
        pl.semaphore_signal(
            barrier, inc=1, device_id={"space": lax.rem(me + s, N)}, device_id_type=MESH
        )
    pl.semaphore_wait(barrier, N - 1)

    def incoming(k, s):
        peer = lax.rem(me + s, N)
        cx, cy = place(peer, k)
        return pltpu.make_async_remote_copy(
            src_ref=vol.at[:, cx, :, cy],
            dst_ref=recv.at[k, pl.ds(2 * me, 2)],
            send_sem=in_send.at[k, s],
            recv_sem=in_recv.at[k, s],
            device_id={"space": peer},
            device_id_type=MESH,
        )

    def incoming_own(k):
        cx, cy = place(me, k)
        return pltpu.make_async_copy(
            vol.at[:, cx, :, cy], recv.at[k, pl.ds(2 * me, 2)], in_own.at[k]
        )

    def outgoing(k, s):
        peer = lax.rem(me + s, N)
        cx, cy = place(me, k)
        return pltpu.make_async_remote_copy(
            src_ref=done.at[k, pl.ds(2 * peer, 2)],
            dst_ref=out.at[:, cx, :, cy],
            send_sem=out_send.at[k, s],
            recv_sem=out_recv.at[k, s],
            device_id={"space": peer},
            device_id_type=MESH,
        )

    def outgoing_own(k):
        cx, cy = place(me, k)
        return pltpu.make_async_copy(
            done.at[k, pl.ds(2 * me, 2)], out.at[:, cx, :, cy], out_own.at[k]
        )

    def arrival(k, s):
        owner = lax.rem(me + N - s, N)
        cx, cy = place(owner, k)
        return pltpu.make_async_remote_copy(
            src_ref=done.at[k, pl.ds(2 * me, 2)],
            dst_ref=out.at[:, cx, :, cy],
            send_sem=out_send.at[k, s],
            recv_sem=out_recv.at[k, s],
            device_id={"space": lax.rem(me + s, N)},
            device_id_type=MESH,
        )

    def landing(k, s):
        owner = lax.rem(me + N - s, N)
        cx, cy = place(me, k)
        return pltpu.make_async_remote_copy(
            src_ref=vol.at[:, cx, :, cy],
            dst_ref=recv.at[k, pl.ds(2 * owner, 2)],
            send_sem=in_send.at[k, s],
            recv_sem=in_recv.at[k, s],
            device_id={"space": lax.rem(me + s, N)},
            device_id_type=MESH,
        )

    for k in range(2):
        incoming_own(k).start()

        @pl.loop(1, N)
        def _(s):
            incoming(k, s).start()

    clear(fine, 1)
    clear(coarse, 2)

    @pl.loop(0, 2)
    def _(k):
        def take(owner):
            for i in range(2):
                x = 2 * owner + i
                fill(fine, x + 1, 1, recv[k, x], 4)

        incoming_own(k).wait()
        take(me)

        @pl.loop(1, N)
        def _(s):
            landing(k, s).wait_recv()
            take(lax.rem(me + N - s, N))

        @pl.loop(0, S)
        def _(x):
            total = taps(fine, x, 1, fw)
            own = fine[x + 1, pl.ds(1, S), :, 256:512].reshape(S * S, 256)
            middle = own.astype(F32) + jax.nn.gelu(total + fb[...])
            fill(coarse, x + 2, 2, middle.astype(jnp.bfloat16).reshape(S, S, 256), 8)

        def finish(x):
            total = taps(coarse, x, 2, cw)
            own = coarse[x + 2, pl.ds(2, S), :, 256:512].reshape(S * S, 256)
            result = own.astype(F32) + jax.nn.gelu(total + cb[...])
            done[k, x] = result.astype(jnp.bfloat16).reshape(S, S, 256)

        @pl.loop(1, N)
        def _(s):
            peer = lax.rem(me + s, N)

            @pl.loop(0, 2)
            def _(i):
                finish(2 * peer + i)

            outgoing(k, s).start()

        @pl.loop(0, 2)
        def _(i):
            finish(2 * me + i)

        outgoing_own(k).start()

    for k in range(2):
        outgoing_own(k).wait()

        @pl.loop(1, N)
        def _(s):
            incoming(k, s).wait_send()
            outgoing(k, s).wait_send()
            arrival(k, s).wait_recv()


def fused(volume, fine_filter, coarse_filter, fine_bias, coarse_bias):
    bf16 = jnp.bfloat16
    fw = filters(fine_filter).reshape(9, 768, 256)
    cw = filters(coarse_filter).reshape(9, 768, 256)
    vmem = pl.BlockSpec(memory_space=pltpu.VMEM)
    hbm = pl.BlockSpec(memory_space=pl.ANY)
    dma = pltpu.SemaphoreType.DMA
    result = pl.pallas_call(
        kernel,
        out_shape=jax.ShapeDtypeStruct((2, 4, S, 4, S, 256), bf16),
        in_specs=[hbm, vmem, vmem, vmem, vmem],
        out_specs=hbm,
        scratch_shapes=[
            pltpu.VMEM((2, S, S, S, 256), bf16),
            pltpu.VMEM((S + 2, S + 2, S, 768), bf16),
            pltpu.VMEM((S + 4, S + 4, S, 768), bf16),
            pltpu.VMEM((2, S, S, S, 256), bf16),
            dma((2, N)), dma((2, N)), dma((2,)),
            dma((2, N)), dma((2, N)), dma((2,)),
        ],
        compiler_params=pltpu.CompilerParams(
            collective_id=0, has_side_effects=True, vmem_limit_bytes=56 * 2**20
        ),
    )(
        volume.reshape(2, 4, S, 4, S, 256), fw, cw,
        fine_bias.reshape(1, 256), coarse_bias.reshape(1, 256),
    )
    return result.reshape(volume.shape)


def on_device(volume, fine_filter, coarse_filter, fine_bias, coarse_bias):
    devices = lax.axis_size("space")
    if devices == N and volume.shape == (1, 1, 8, 64, 16, 256):
        return fused(volume, fine_filter, coarse_filter, fine_bias, coarse_bias)
    brick = volume[0, 0]
    fine_weights = filters(fine_filter)
    coarse_weights = filters(coarse_filter)
    cosets = fine_cosets(brick)
    outgoing = cosets.reshape((devices, 64 // devices, 1) + cosets.shape[1:])
    received = lax.all_to_all(outgoing, "space", split_axis=0, concat_axis=2, tiled=True)
    items = received.shape[1]
    along_u = received.shape[3]
    along_v = received.shape[4]
    grid = dense_taps(assemble(received[0]), fine_weights, fine_bias)
    finer = dense_taps(split_halves(grid), coarse_weights, coarse_bias)
    grid = join_halves(finer, items)
    returned = lax.all_to_all(
        disassemble(grid, along_u, along_v), "space", split_axis=2, concat_axis=0, tiled=True
    )
    brick = fine_bricks(returned.reshape(cosets.shape))
    return brick.reshape(volume.shape)


def solution(mesh):
    return jax.shard_map(
        on_device,
        mesh=mesh,
        in_specs=(
            P("dp", "space", None, None, None, None),
            P(None, None, None, "dp", None),
            P(None, None, None, "dp", None),
            P(),
            P(),
        ),
        out_specs=P("dp", "space", None, None, None, None),
        check_vma=False,
    )
```

```python
import jax
import jax.numpy as jnp
from jax import lax
from jax.experimental import pallas as pl
from jax.experimental.pallas import tpu as pltpu
from jax.sharding import PartitionSpec as P

X = 64
BX = 8


def filters(shard):
    return lax.all_gather(shard, "dp", axis=3, tiled=True)


def dense_taps(grid, weights, bias):
    items, length_x, length_y, length_z, channels = grid.shape
    padded = jnp.pad(grid, ((0, 0), (1, 1), (1, 1), (1, 1), (0, 0)))
    total = jnp.zeros(grid.shape, jnp.float32)
    for step_x in range(3):
        for step_y in range(3):
            window = padded[:, step_x : step_x + length_x, step_y : step_y + length_y]
            stacked = jnp.concatenate(
                [window[:, :, :, depth : depth + length_z] for depth in range(3)], axis=-1
            )
            total = total + jnp.dot(
                stacked,
                weights[step_x, step_y].reshape(3 * channels, channels),
                preferred_element_type=jnp.float32,
            )
    return (grid.astype(jnp.float32) + jax.nn.gelu(total + bias)).astype(jnp.bfloat16)


def fine_cosets(brick):
    size_x, size_y, size_z, channels = brick.shape
    split = brick.reshape(size_x // 4, 4, size_y // 4, 4, size_z // 4, 4, channels)
    return split.transpose(1, 3, 5, 0, 2, 4, 6).reshape(
        64, size_x // 4, size_y // 4, size_z // 4, channels
    )


def fine_bricks(cosets):
    count, along_u, along_v, along_w, channels = cosets.shape
    split = cosets.reshape(4, 4, 4, along_u, along_v, along_w, channels).transpose(
        3, 0, 4, 1, 5, 2, 6
    )
    return split.reshape(along_u * 4, along_v * 4, along_w * 4, channels)


def assemble(parts):
    items, devices, along_u, along_v, along_w, channels = parts.shape
    across_x = X // BX
    across_y = devices // across_x
    grid = parts.reshape(items, across_x, across_y, along_u, along_v, along_w, channels).transpose(
        0, 1, 3, 2, 4, 5, 6
    )
    return grid.reshape(items, across_x * along_u, across_y * along_v, along_w, channels)


def disassemble(grid, along_u, along_v):
    items, size_x, size_y, along_w, channels = grid.shape
    across_x = size_x // along_u
    across_y = size_y // along_v
    parts = grid.reshape(items, across_x, along_u, across_y, along_v, along_w, channels).transpose(
        0, 1, 3, 2, 4, 5, 6
    )
    return parts.reshape(1, items, across_x * across_y, along_u, along_v, along_w, channels)


def split_halves(grid):
    items, size_x, size_y, size_z, channels = grid.shape
    parts = grid.reshape(items, size_x // 2, 2, size_y // 2, 2, size_z // 2, 2, channels).transpose(
        0, 2, 4, 6, 1, 3, 5, 7
    )
    return parts.reshape(items * 8, size_x // 2, size_y // 2, size_z // 2, channels)


def join_halves(parts, items):
    count, half_x, half_y, half_z, channels = parts.shape
    grid = parts.reshape(items, 2, 2, 2, half_x, half_y, half_z, channels).transpose(
        0, 4, 1, 5, 2, 6, 3, 7
    )
    return grid.reshape(items, half_x * 2, half_y * 2, half_z * 2, channels)


MESH = pl.DeviceIdType.MESH
N = 8
S = 16
F32 = jnp.float32


def place(owner, k):
    number = 2 * owner + k
    return lax.div(number, 4), lax.rem(number, 4)


def spread(rows, shift):
    zero = jnp.zeros((S, shift, rows.shape[-1]), F32)
    before = jnp.concatenate([zero, rows[:, : S - shift]], axis=1)
    after = jnp.concatenate([rows[:, shift:], zero], axis=1)
    return before.astype(jnp.bfloat16), after.astype(jnp.bfloat16)


def taps(grid, x, step, weights):
    acc = None
    for dx in range(3):
        for dy in range(3):
            lhs = grid[x + dx * step, pl.ds(dy * step, S)].reshape(S * S, 768)
            rhs = weights[9 * dx + 3 * dy : 9 * dx + 3 * dy + 3].reshape(768, 256)
            part = jnp.dot(lhs, rhs, preferred_element_type=F32)
            acc = part if acc is None else acc + part
    return acc


def fill(grid, x, pad, rows, shift):
    before, after = spread(rows.astype(F32), shift)
    grid[x, pl.ds(pad, S), :, 0:256] = before
    grid[x, pl.ds(pad, S), :, 256:512] = rows
    grid[x, pl.ds(pad, S), :, 512:768] = after


def clear(grid, pad):
    side = S + 2 * pad
    for edge in list(range(pad)) + list(range(S + pad, side)):
        grid[edge] = jnp.zeros((side, S, 768), jnp.bfloat16)

    @pl.loop(pad, S + pad)
    def _(x):
        grid[x, 0:pad] = jnp.zeros((pad, S, 768), jnp.bfloat16)
        grid[x, S + pad : side] = jnp.zeros((pad, S, 768), jnp.bfloat16)


def kernel(
    vol, fs, cs, fb, cb, out, recv, fine, coarse, done, fw, cw,
    in_send, in_recv, in_own, out_send, out_recv, out_own,
    hop_send, hop_recv, twin_send, twin_recv, shard_own,
):
    me = lax.axis_index("space")
    z = lax.axis_index("dp")
    core = lax.rem(me, 2)
    twin = me + 1 - 2 * core
    shards, weights = (fs, cs), (fw, cw)
    depth = fs.shape[1]
    half = depth // 2
    layers = 256 // depth

    barrier = pltpu.get_barrier_semaphore()
    for s in range(1, N):
        pl.semaphore_signal(
            barrier, inc=1, device_id={"space": lax.rem(me + s, N)}, device_id_type=MESH
        )
    for s in range(1, layers):
        pl.semaphore_signal(
            barrier, inc=1, device_id={"dp": lax.rem(z + s, layers)}, device_id_type=MESH
        )
    pl.semaphore_wait(barrier, N - 1 + layers - 1)

    def rows(f, owner, which):
        start = pl.multiple_of(owner * depth + which * half, half)
        return weights[f].at[:, pl.ds(start, half)]

    def valid(owner):
        return (owner >= 0) & (owner < layers)

    def hop(f, way, t):
        sign = 1 - 2 * way
        target = rows(f, z - sign * t, core)
        source = target
        if t == 0:
            source = shards[f].at[:, pl.ds(pl.multiple_of(core * half, half), half)]
        return pltpu.make_async_remote_copy(
            src_ref=source,
            dst_ref=target,
            send_sem=hop_send.at[f, way, t],
            recv_sem=hop_recv.at[f, way, t],
            device_id={"dp": z + sign},
            device_id_type=MESH,
        )

    def hop_landing(f, way, t):
        sign = 1 - 2 * way
        target = rows(f, z - sign * (t + 1), core)
        return pltpu.make_async_remote_copy(
            src_ref=target,
            dst_ref=target,
            send_sem=hop_send.at[f, way, t],
            recv_sem=hop_recv.at[f, way, t],
            device_id={"dp": z - sign},
            device_id_type=MESH,
        )

    def pass_on(f, way, t, which):
        sign = 1 - 2 * way
        target = rows(f, z - sign * (t + 1), which)
        return pltpu.make_async_remote_copy(
            src_ref=target,
            dst_ref=target,
            send_sem=twin_send.at[f, way, t],
            recv_sem=twin_recv.at[f, way, t],
            device_id={"space": twin},
            device_id_type=MESH,
        )

    def shard_copy(f):
        start = pl.multiple_of(z * depth, depth)
        return pltpu.make_async_copy(
            shards[f], weights[f].at[:, pl.ds(start, depth)], shard_own.at[f]
        )

    def send_shard(f):
        for way in range(2):
            @pl.when(valid(z + 1 - 2 * way))
            def _():
                hop(f, way, 0).start()

    def relay(f, t):
        for way in range(2):
            sign = 1 - 2 * way

            @pl.when(valid(z - sign * (t + 1)))
            def _():
                hop_landing(f, way, t).wait_recv()
                if t + 1 < layers - 1:
                    @pl.when(valid(z + sign))
                    def _():
                        hop(f, way, t + 1).start()
                pass_on(f, way, t, core).start()

    def gathered(f):
        shard_copy(f).wait()
        for way in range(2):
            for t in range(layers - 1):
                @pl.when(valid(z - (1 - 2 * way) * (t + 1)))
                def _():
                    pass_on(f, way, t, 1 - core).wait_recv()

    def all_sent(f):
        for way in range(2):
            sign = 1 - 2 * way
            for t in range(layers - 1):
                @pl.when(valid(z - sign * t) & valid(z + sign))
                def _():
                    hop(f, way, t).wait_send()

                @pl.when(valid(z - sign * (t + 1)))
                def _():
                    pass_on(f, way, t, core).wait_send()

    def incoming(k, s):
        peer = lax.rem(me + s, N)
        cx, cy = place(peer, k)
        return pltpu.make_async_remote_copy(
            src_ref=vol.at[:, cx, :, cy],
            dst_ref=recv.at[k, pl.ds(2 * me, 2)],
            send_sem=in_send.at[k, s],
            recv_sem=in_recv.at[k, s],
            device_id={"space": peer},
            device_id_type=MESH,
        )

    def incoming_own(k):
        cx, cy = place(me, k)
        return pltpu.make_async_copy(
            vol.at[:, cx, :, cy], recv.at[k, pl.ds(2 * me, 2)], in_own.at[k]
        )

    def outgoing(k, s):
        peer = lax.rem(me + s, N)
        cx, cy = place(me, k)
        return pltpu.make_async_remote_copy(
            src_ref=done.at[k, pl.ds(2 * peer, 2)],
            dst_ref=out.at[:, cx, :, cy],
            send_sem=out_send.at[k, s],
            recv_sem=out_recv.at[k, s],
            device_id={"space": peer},
            device_id_type=MESH,
        )

    def outgoing_own(k):
        cx, cy = place(me, k)
        return pltpu.make_async_copy(
            done.at[k, pl.ds(2 * me, 2)], out.at[:, cx, :, cy], out_own.at[k]
        )

    def arrival(k, s):
        owner = lax.rem(me + N - s, N)
        cx, cy = place(owner, k)
        return pltpu.make_async_remote_copy(
            src_ref=done.at[k, pl.ds(2 * me, 2)],
            dst_ref=out.at[:, cx, :, cy],
            send_sem=out_send.at[k, s],
            recv_sem=out_recv.at[k, s],
            device_id={"space": lax.rem(me + s, N)},
            device_id_type=MESH,
        )

    def landing(k, s):
        owner = lax.rem(me + N - s, N)
        cx, cy = place(me, k)
        return pltpu.make_async_remote_copy(
            src_ref=vol.at[:, cx, :, cy],
            dst_ref=recv.at[k, pl.ds(2 * owner, 2)],
            send_sem=in_send.at[k, s],
            recv_sem=in_recv.at[k, s],
            device_id={"space": lax.rem(me + s, N)},
            device_id_type=MESH,
        )

    send_shard(0)
    for k in range(2):
        incoming_own(k).start()

        @pl.loop(1, N)
        def _(s):
            incoming(k, s).start()

    shard_copy(0).start()
    shard_copy(1).start()
    clear(fine, 1)
    clear(coarse, 2)
    for t in range(layers - 1):
        relay(0, t)
        if t == layers - 3:
            send_shard(1)

    @pl.loop(0, 2)
    def _(k):
        def take(owner):
            for i in range(2):
                x = 2 * owner + i
                fill(fine, x + 1, 1, recv[k, x], 4)

        incoming_own(k).wait()
        take(me)

        @pl.loop(1, N)
        def _(s):
            landing(k, s).wait_recv()
            take(lax.rem(me + N - s, N))

        @pl.when(k == 0)
        def _():
            gathered(0)

        @pl.loop(0, S)
        def _(x):
            for t in range(layers - 1):
                @pl.when((k == 0) & (x == 5 + 5 * t))
                def _():
                    relay(1, t)

            total = taps(fine, x, 1, fw)
            own = fine[x + 1, pl.ds(1, S), :, 256:512].reshape(S * S, 256)
            middle = own.astype(F32) + jax.nn.gelu(total + fb[...])
            fill(coarse, x + 2, 2, middle.astype(jnp.bfloat16).reshape(S, S, 256), 8)

        @pl.when(k == 0)
        def _():
            gathered(1)

        def finish(x):
            total = taps(coarse, x, 2, cw)
            own = coarse[x + 2, pl.ds(2, S), :, 256:512].reshape(S * S, 256)
            result = own.astype(F32) + jax.nn.gelu(total + cb[...])
            done[k, x] = result.astype(jnp.bfloat16).reshape(S, S, 256)

        @pl.loop(1, N)
        def _(s):
            peer = lax.rem(me + s, N)

            @pl.loop(0, 2)
            def _(i):
                finish(2 * peer + i)

            outgoing(k, s).start()

        @pl.loop(0, 2)
        def _(i):
            finish(2 * me + i)

        outgoing_own(k).start()

    all_sent(0)
    all_sent(1)
    for k in range(2):
        outgoing_own(k).wait()

        @pl.loop(1, N)
        def _(s):
            incoming(k, s).wait_send()
            outgoing(k, s).wait_send()
            arrival(k, s).wait_recv()


def fused(volume, fine_filter, coarse_filter, fine_bias, coarse_bias):
    bf16 = jnp.bfloat16
    depth = fine_filter.shape[3]
    layers = 256 // depth
    vmem = pl.BlockSpec(memory_space=pltpu.VMEM)
    hbm = pl.BlockSpec(memory_space=pl.ANY)
    dma = pltpu.SemaphoreType.DMA
    result = pl.pallas_call(
        kernel,
        out_shape=jax.ShapeDtypeStruct((2, 4, S, 4, S, 256), bf16),
        in_specs=[hbm, hbm, hbm, vmem, vmem],
        out_specs=hbm,
        scratch_shapes=[
            pltpu.VMEM((2, S, S, S, 256), bf16),
            pltpu.VMEM((S + 2, S + 2, S, 768), bf16),
            pltpu.VMEM((S + 4, S + 4, S, 768), bf16),
            pltpu.VMEM((2, S, S, S, 256), bf16),
            pltpu.VMEM((27, 256, 256), bf16),
            pltpu.VMEM((27, 256, 256), bf16),
            dma((2, N)), dma((2, N)), dma((2,)),
            dma((2, N)), dma((2, N)), dma((2,)),
            dma((2, 2, layers - 1)), dma((2, 2, layers - 1)),
            dma((2, 2, layers - 1)), dma((2, 2, layers - 1)), dma((2,)),
        ],
        compiler_params=pltpu.CompilerParams(
            collective_id=0, has_side_effects=True, vmem_limit_bytes=56 * 2**20
        ),
    )(
        volume.reshape(2, 4, S, 4, S, 256),
        fine_filter.reshape(27, depth, 256), coarse_filter.reshape(27, depth, 256),
        fine_bias.reshape(1, 256), coarse_bias.reshape(1, 256),
    )
    return result.reshape(volume.shape)


def on_device(volume, fine_filter, coarse_filter, fine_bias, coarse_bias):
    devices = lax.axis_size("space")
    fits = devices == N and lax.axis_size("dp") == 4
    if fits and volume.shape == (1, 1, 8, 64, 16, 256):
        return fused(volume, fine_filter, coarse_filter, fine_bias, coarse_bias)
    brick = volume[0, 0]
    fine_weights = filters(fine_filter)
    coarse_weights = filters(coarse_filter)
    cosets = fine_cosets(brick)
    outgoing = cosets.reshape((devices, 64 // devices, 1) + cosets.shape[1:])
    received = lax.all_to_all(outgoing, "space", split_axis=0, concat_axis=2, tiled=True)
    items = received.shape[1]
    along_u = received.shape[3]
    along_v = received.shape[4]
    grid = dense_taps(assemble(received[0]), fine_weights, fine_bias)
    finer = dense_taps(split_halves(grid), coarse_weights, coarse_bias)
    grid = join_halves(finer, items)
    returned = lax.all_to_all(
        disassemble(grid, along_u, along_v), "space", split_axis=2, concat_axis=0, tiled=True
    )
    brick = fine_bricks(returned.reshape(cosets.shape))
    return brick.reshape(volume.shape)


def solution(mesh):
    return jax.shard_map(
        on_device,
        mesh=mesh,
        in_specs=(
            P("dp", "space", None, None, None, None),
            P(None, None, None, "dp", None),
            P(None, None, None, "dp", None),
            P(),
            P(),
        ),
        out_specs=P("dp", "space", None, None, None, None),
        check_vma=False,
    )
```
